256 devices in a mesh: py: 16 (over z_hi, y), pz: 16 (over x, z_lo, core).
Axes of the slice: x: 4, y: 4, z: 8 (z_hi: 4, z_lo: 2; z = z_hi * 2 + z_lo), core: 2. Of those that a mesh axis runs over, the one named last changes fastest.
Arguments:
- solid: int32 [256, 512, 512], P('py', 'pz'), may hold values 0 or 1
- orientation: float32 [256, 512, 512], P('py', 'pz'), may hold values from -6 to 6
Outputs:
- power_solid: float32 [512, 512, 256], P('py', 'pz')
- power_orient: float32 [512, 512, 256], P('py', 'pz')
- cross: float32 [2, 512, 512, 256], P(None, 'py', 'pz')
The draws below stay inside these ranges and needn't reach their ends.
Inputs may be any that keep to these rules, and one draw needn't show every extreme that they name: 0 marks pore space, 1 marks solid.
All inputs are finite; a program needn't handle non-finite values. No bound on the sum of `solid` on one device may be relied on, other than what follows from the above.
Results may differ from the reference program's by a relative error of at most 0.0003.
Values sent between devices are 32-bit elements; how exact they have to be, the bound alone decides.
No kernel may reach another device: no remote copies, remote signals or barrier semaphores. Data moves between devices by JAX's collectives and lax.ppermute only.
A program may use at most 128 MiB of HBM per device.

```python
import jax
import jax.numpy as jnp

NX = 256
NY = 512
NZ = 512


def touch_ends(values, own_key, smallest, top_value):
    extent = values.shape
    place = [jax.random.randint(jax.random.fold_in(own_key, axis), (), 0, extent[axis]) for axis in range(len(extent))]
    values = values.at[tuple(place)].set(smallest)
    longest = extent.index(max(extent))
    place[longest] = (place[longest] + 1) % extent[longest]
    return values.at[tuple(place)].set(top_value)


def block_scale(stream_key, extent, shards, smallest, largest):
    gain, own = 1.0, jax.random.fold_in(stream_key, 6)
    for axis_at, blocks in shards:
        steps = jnp.exp(jax.random.uniform(jax.random.fold_in(own, axis_at), (blocks,), jnp.float32, smallest / len(shards), largest / len(shards)))
        gain = gain * jnp.repeat(steps, extent[axis_at] // blocks).reshape([-1 if axis == axis_at else 1 for axis in range(len(extent))])
    return gain


def bell_draw(rng, shape, spread, bound, shards=(), kind=jnp.bfloat16):
    array = spread * jax.random.normal(rng, shape, jnp.float32)
    if shards:
        array = array * block_scale(rng, shape, shards, -0.22, 0.18)
    return jnp.clip(array, -bound, bound).astype(kind)


def setup_inputs(seed: int = 0) -> dict:
    arg_keys = jax.random.split(jax.random.key(seed), 3)
    return {
        "solid": touch_ends((jax.random.randint(arg_keys[0], (NX, NY, NZ), 0, 3) < 1).astype(jnp.int32), jax.random.fold_in(arg_keys[0], 1), 0, 1),
        "orientation": bell_draw(arg_keys[1], (NX, NY, NZ), 1.0, 6.0, ((0, 16), (1, 16)), jnp.float32),
    }


def signed_freq(length):
    counter = jnp.arange(length, dtype=jnp.int32)
    shifted = (counter + length // 2) % length - length // 2
    return shifted.astype(jnp.float32) / (length / 2.0)


def reference(solid, orientation):
    packed = solid.astype(jnp.float32) + 1j * orientation
    spectrum = jnp.fft.fftn(packed)
    mirrored = jnp.roll(jnp.flip(spectrum), 1, axis=(0, 1, 2))
    spec_re = jnp.real(spectrum)
    spec_im = jnp.imag(spectrum)
    mirr_re = jnp.real(mirrored)
    mirr_im = jnp.imag(mirrored)
    solid_re = (spec_re + mirr_re) / 2.0
    solid_im = (spec_im - mirr_im) / 2.0
    orient_re = (spec_im + mirr_im) / 2.0
    orient_im = (mirr_re - spec_re) / 2.0
    freq_x = signed_freq(NX)
    freq_y = signed_freq(NY)
    freq_z = signed_freq(NZ)
    weight = jnp.exp(-0.5 * (freq_x[:, None, None] ** 2 + freq_y[None, :, None] ** 2 + freq_z[None, None, :] ** 2))
    weight = weight.at[0, 0, 0].set(0.0)
    scaled = weight / (NX * NY * NZ)
    power_solid = scaled * (solid_re * solid_re + solid_im * solid_im)
    power_orient = scaled * (orient_re * orient_re + orient_im * orient_im)
    cross_re = scaled * (solid_re * orient_re + solid_im * orient_im)
    cross_im = scaled * (solid_im * orient_re - solid_re * orient_im)
    order = (1, 2, 0)
    return (jnp.transpose(power_solid, order), jnp.transpose(power_orient, order),
            jnp.stack([jnp.transpose(cross_re, order), jnp.transpose(cross_im, order)]))
```

```python
import jax
import jax.numpy as jnp
import numpy as np
from jax import lax
from jax.experimental import pallas as pl
from jax.experimental.pallas import tpu as pltpu
from jax.sharding import PartitionSpec as P

F32 = jnp.float32
BF16 = jnp.bfloat16
LANES = 128
VMEM_LIMIT = 56 * 1024 * 1024


def two_parts(table):
    high = np.asarray(table, np.float32).astype(jnp.bfloat16)
    low = (np.asarray(table, np.float64) - high.astype(np.float64)).astype(np.float32).astype(jnp.bfloat16)
    return high, low


def cos_sin(rows, columns, length):
    angles = (np.outer(rows, columns) % length) * (2.0 * np.pi / length)
    return np.cos(angles), np.sin(angles)


def first_kz(place):
    return 32 * place if place < 8 else 32 * (15 - place) + 16


def z_tables():
    z = np.arange(512)
    regular, extra = [], []
    for place in range(16):
        cos, sin = cos_sin(z, first_kz(place) + np.arange(17), 512)
        regular += [cos[:, :16], -sin[:, :16]]
        extra += [cos[:, 16:], -sin[:, 16:]]
    return two_parts(np.concatenate(regular + extra * 4, 1))


def y_tables():
    n = np.arange(512)
    cos, sin = cos_sin(n, n, 512)
    return two_parts(np.concatenate([cos, sin], 0))


def x_tables():
    half, source, low = np.meshgrid(np.arange(2), np.arange(16), np.arange(8), indexing="ij")
    x = (source * 16 + half * 8 + low).reshape(-1)
    cos, sin = cos_sin(x, np.arange(256), 256)
    return two_parts(np.concatenate([cos, sin], 1))


def split(values):
    high = values.astype(BF16)
    return high, (values - high.astype(F32)).astype(BF16)


def dot(a, b):
    return jnp.dot(a, b, preferred_element_type=F32)


def lane_of(shape):
    return lax.broadcasted_iota(jnp.int32, shape, len(shape) - 1)


def permuted(values, source_lane):
    return jnp.take_along_axis(values, source_lane, axis=1, mode="promise_in_bounds")


def z_kernel(solid_ref, orient_ref, high_ref, low_ref, out_ref):
    size_y = solid_ref.shape[1]
    rows = 8 * size_y
    high, low = high_ref[...], low_ref[...]
    solid = solid_ref[...].reshape(2 * rows, 512).astype(F32).astype(BF16)
    orient, rest = split(orient_ref[...].reshape(2 * rows, 512))
    solid_z = dot(solid, high) + dot(solid, low)
    orient_z = dot(orient, high) + (dot(orient, low) + dot(rest, high))
    pieces = (solid_z[:rows], orient_z[:rows], solid_z[rows:], orient_z[rows:])
    lane = lane_of((rows, LANES))
    group = lane // 32

    def gathered(parts):
        return jnp.where(group == 0, parts[0], jnp.where(group == 1, parts[1], jnp.where(group == 2, parts[2], parts[3])))

    for tile in range(4):
        columns = [piece[:, LANES * tile : LANES * (tile + 1)] for piece in pieces]
        for q in range(4):
            moved = [columns[c] if c == q else pltpu.roll(columns[c], 32 * (c - q) % LANES, 1) for c in range(4)]
            out_ref[4 * tile + q, 0:8] = gathered(moved).reshape(8, size_y, LANES)
    extra = gathered([piece[:, 512:640] for piece in pieces])
    spot = lane_of((size_y, LANES)) % 16
    for place in range(16):
        spread = permuted(extra, group * 32 + 2 * place + lane // 16 % 2)
        total = jnp.zeros((size_y, LANES), F32)
        for k in range(8):
            total = jnp.where(spot == k, spread[k * size_y : (k + 1) * size_y], total)
        out_ref[place, 8] = total


def y_kernel(data_ref, extra_ref, high_ref, low_ref, out_ref, extra_y_ref):
    high, low = high_ref[...], low_ref[...]
    lane = lane_of((512, LANES))
    sign = jnp.where(lane // 16 % 2 == 0, 1.0, -1.0).astype(F32)
    swap = lane ^ 16
    back = lane // 16 * 16 + (16 - lane % 16) % 16

    def transformed(values):
        first, rest = split(values)
        return dot(high, first) + (dot(high, rest) + dot(low, first))

    def turned(products):
        return permuted(products, swap) * sign

    @pl.when(pl.program_id(0) == 0)
    def _():
        products = transformed(extra_ref[...].reshape(512, LANES))
        extra_y_ref[...] = (products[:512] - turned(products[512:])) * sign

    per_step = data_ref.shape[1]
    values = jnp.concatenate([data_ref[:, k].reshape(512, LANES) for k in range(per_step)], 1)
    products = transformed(values)
    for k in range(per_step):
        cos_part = products[:512, LANES * k : LANES * (k + 1)]
        sin_part = turned(products[512:, LANES * k : LANES * (k + 1)])
        out_ref[:, 0, k] = (cos_part + sin_part).reshape(16, 32, LANES)
        mirrored = permuted((cos_part - sin_part) * sign, back)
        x8 = pl.program_id(0) * per_step + k
        border = pltpu.roll(extra_y_ref[...], (LANES - x8) % LANES, 1)
        out_ref[:, 1, k] = jnp.where(lane % 16 == 0, border, mirrored).reshape(16, 32, LANES)


def signed_freq(counter, length):
    shifted = (counter + length // 2) % length - length // 2
    return shifted.astype(F32) / (length / 2.0)


def x_kernel(place_ref, data_ref, high_ref, low_ref, solid_ref, orient_ref, cross_ref, first_ref, rest_ref):
    size_y = solid_ref.shape[0]
    pz = place_ref[1]
    flip = (pz >= 8).astype(jnp.int32)
    for ky in range(size_y):
        for half in range(2):
            rows = [data_ref[source, half ^ flip, pl.ds(ky, 8, stride=size_y), :] for source in range(16)]
            turned = jnp.concatenate(rows, 0).T
            joined = jnp.concatenate([turned[:64], turned[64:]], 1)
            first, rest = split(joined)
            start = ky * 128 + half * 64
            first_ref[start : start + 64] = first
            rest_ref[start : start + 64] = rest
    high, low = high_ref[...], low_ref[...]
    products = dot(first_ref[...], high) + (dot(first_ref[...], low) + dot(rest_ref[...], high))

    kx = lax.broadcasted_iota(jnp.int32, (32, 256), 1)
    kz = lax.broadcasted_iota(jnp.int32, (32, 256), 0) + pz * 32
    freq = signed_freq(kx, 256) ** 2 + signed_freq(kz, 512) ** 2
    plane = jnp.exp(-0.5 * freq) * (1.0 / 67108864.0)
    first_ky = place_ref[0] * 32 + pl.program_id(0) * size_y
    for ky in range(size_y):
        index = jnp.full((32, 256), first_ky + ky, jnp.int32)
        weight = plane * jnp.exp(-0.5 * signed_freq(index[:1], 512) ** 2)
        weight = jnp.where((kx == 0) & (kz == 0) & (index == 0), 0.0, weight)
        for half in range(2):
            start = ky * 128 + half * 64
            cos_part = [products[start + 16 * i : start + 16 * (i + 1), :256] for i in range(4)]
            sin_part = [products[start + 16 * i : start + 16 * (i + 1), 256:] for i in range(4)]
            solid_re = cos_part[0] + sin_part[1]
            solid_im = cos_part[1] - sin_part[0]
            orient_re = cos_part[2] + sin_part[3]
            orient_im = cos_part[3] - sin_part[2]
            scaled = weight[16 * half : 16 * (half + 1)]
            where = pl.ds(16 * half, 16)
            solid_ref[ky, where] = scaled * (solid_re * solid_re + solid_im * solid_im)
            orient_ref[ky, where] = scaled * (orient_re * orient_re + orient_im * orient_im)
            cross_ref[0, ky, where] = scaled * (solid_re * orient_re + solid_im * orient_im)
            cross_ref[1, ky, where] = scaled * (solid_im * orient_re - solid_re * orient_im)


def whole(shape):
    return pl.BlockSpec(shape, lambda *_: (0,) * len(shape))


def body(solid, orientation):
    params = pltpu.CompilerParams(vmem_limit_bytes=VMEM_LIMIT, dimension_semantics=("arbitrary",))
    z_high, z_low = z_tables()
    step_y = 8
    field = pl.pallas_call(
        z_kernel,
        grid=(32 // step_y,),
        in_specs=[
            pl.BlockSpec((16, step_y, 512), lambda i: (0, i, 0)),
            pl.BlockSpec((16, step_y, 512), lambda i: (0, i, 0)),
            whole(z_high.shape),
            whole(z_low.shape),
        ],
        out_specs=pl.BlockSpec((16, 9, step_y, LANES), lambda i: (0, 0, i, 0)),
        out_shape=jax.ShapeDtypeStruct((16, 9, 32, LANES), F32),
        compiler_params=params,
        name="z_transform",
    )(solid, orientation, z_high, z_low)
    field = lax.all_to_all(field.reshape(16, 9 * 32, LANES), "pz", 0, 0, tiled=True).reshape(16, 9, 32, LANES)

    y_high, y_low = y_tables()
    per_step = 2
    field = pl.pallas_call(
        y_kernel,
        grid=(8 // per_step,),
        in_specs=[
            pl.BlockSpec((16, per_step, 32, LANES), lambda i: (0, i, 0, 0)),
            pl.BlockSpec((16, 1, 32, LANES), lambda i: (0, 8, 0, 0)),
            whole(y_high.shape),
            whole(y_low.shape),
        ],
        out_specs=pl.BlockSpec((16, 2, per_step, 32, LANES), lambda i: (0, 0, i, 0, 0)),
        out_shape=jax.ShapeDtypeStruct((16, 2, 8, 32, LANES), F32),
        scratch_shapes=[pltpu.VMEM((512, LANES), F32)],
        compiler_params=params,
        name="y_transform",
    )(field, field, y_high, y_low)
    groups = [[py * 16 + pz for py in range(16) for pz in (low, 15 - low)] for low in range(8)]
    field = lax.all_to_all(
        field.reshape(32, 8 * 32, LANES), ("py", "pz"), 0, 0, tiled=True, axis_index_groups=groups
    ).reshape(16, 2, 8, 32, LANES)

    x_high, x_low = x_tables()
    step_ky = 8
    place = jnp.stack([lax.axis_index("py"), lax.axis_index("pz")]).astype(jnp.int32)
    out_spec = pl.BlockSpec((step_ky, 32, 256), lambda i: (i, 0, 0))
    cross_spec = pl.BlockSpec((2, step_ky, 32, 256), lambda i: (0, i, 0, 0))
    out = jax.ShapeDtypeStruct((32, 32, 256), F32)

    def with_rows(place_ref, data_ref, *refs):
        x_kernel(place_ref, data_ref.reshape(16, 2, 8 * step_ky, LANES), *refs)

    return tuple(
        pl.pallas_call(
            with_rows,
            grid=(32 // step_ky,),
            in_specs=[
                pl.BlockSpec(memory_space=pltpu.SMEM),
                pl.BlockSpec((16, 2, 8, step_ky, LANES), lambda i: (0, 0, 0, i, 0)),
                whole(x_high.shape),
                whole(x_low.shape),
            ],
            out_specs=[out_spec, out_spec, cross_spec],
            out_shape=[out, out, jax.ShapeDtypeStruct((2, 32, 32, 256), F32)],
            scratch_shapes=[pltpu.VMEM((step_ky * 128, 256), BF16)] * 2,
            compiler_params=params,
            name="x_transform",
        )(place, field, x_high, x_low)
    )


def solution(mesh):
    placed = (P("py", "pz", None), P("py", "pz", None))
    return jax.shard_map(
        body,
        mesh=mesh,
        in_specs=placed,
        out_specs=(P("py", "pz", None), P("py", "pz", None), P(None, "py", "pz", None)),
        check_vma=False,
    )
```

```python
import jax
import jax.numpy as jnp
import numpy as np
from jax import lax
from jax.experimental import pallas as pl
from jax.experimental.pallas import tpu as pltpu
from jax.sharding import PartitionSpec as P

F32 = jnp.float32
BF16 = jnp.bfloat16
LANES = 128
VMEM_LIMIT = 36 * 1024 * 1024
STEP_Y = 8
STEP_KY = 8


def two_parts(table):
    high = np.asarray(table, np.float32).astype(jnp.bfloat16)
    low = (np.asarray(table, np.float64) - high.astype(np.float64)).astype(np.float32).astype(jnp.bfloat16)
    return high, low


def cos_sin(rows, columns, length):
    angles = (np.outer(rows, columns) % length) * (2.0 * np.pi / length)
    return np.cos(angles), np.sin(angles)


def first_kz(place):
    return 32 * place if place < 8 else 32 * (15 - place) + 16


def z_tables():
    z = np.arange(512)
    regular, extra = [], []
    for place in range(16):
        cos, sin = cos_sin(z, first_kz(place) + np.arange(17), 512)
        regular += [cos[:, :16], -sin[:, :16]]
        extra += [cos[:, 16:], -sin[:, 16:]]
    return two_parts(np.concatenate(regular + extra * 4, 1))


def y_tables():
    n = np.arange(512)
    cos, sin = cos_sin(n, n, 512)
    return two_parts(np.concatenate([cos, sin], 0))


def x_tables():
    half, source, low = np.meshgrid(np.arange(2), np.arange(16), np.arange(8), indexing="ij")
    x = (source * 16 + half * 8 + low).reshape(-1)
    cos, sin = cos_sin(x, np.arange(256), 256)
    return two_parts(np.concatenate([cos, sin], 1))


def split(values):
    high = values.astype(BF16)
    return high, (values - high.astype(F32)).astype(BF16)


def dot(a, b):
    return jnp.dot(a, b, preferred_element_type=F32)


def lane_of(shape):
    return lax.broadcasted_iota(jnp.int32, shape, len(shape) - 1)


def permuted(values, source_lane):
    return jnp.take_along_axis(values, source_lane, axis=1, mode="promise_in_bounds")


def z_kernel(solid_ref, orient_ref, high_ref, low_ref, out_ref):
    size_y = STEP_Y
    rows = 8 * size_y
    chunks = 32 // size_y
    i = pl.program_id(0)
    high, low = high_ref[...], low_ref[...]
    lane = lane_of((rows, LANES))
    group = lane // 32

    def gathered(items):
        return jnp.where(group == 0, items[0], jnp.where(group == 1, items[1], jnp.where(group == 2, items[2], items[3])))

    spot = lane_of((size_y, LANES)) % 16
    solid = solid_ref[...].reshape(2 * rows, 512).astype(F32).astype(BF16)
    orient, rest = split(orient_ref[...].reshape(2 * rows, 512))
    solid_z = dot(solid, high) + dot(solid, low)
    orient_z = dot(orient, high) + (dot(orient, low) + dot(rest, high))
    pieces = (solid_z[:rows], orient_z[:rows], solid_z[rows:], orient_z[rows:])
    first = pl.multiple_of(i * size_y, 8)
    for tile in range(4):
        columns = [piece[:, LANES * tile : LANES * (tile + 1)] for piece in pieces]
        for q in range(4):
            moved = [columns[c] if c == q else pltpu.roll(columns[c], 32 * (c - q) % LANES, 1) for c in range(4)]
            ready = gathered(moved)
            for k in range(8):
                out_ref[4 * tile + q, pl.ds(32 * k + first, size_y)] = ready[k * size_y : (k + 1) * size_y]
    extra = gathered([piece[:, 512:640] for piece in pieces])
    shift = 8 * (2 * i // chunks)
    place_rows = pl.ds(pl.multiple_of(256 + i * size_y % 16, 8), size_y)
    for place in range(16):
        spread = permuted(extra, group * 32 + 2 * place + lane // 16 % 2)
        total = jnp.where(shift == 0, 0.0, out_ref[place, place_rows])
        for k in range(8):
            total = jnp.where(spot == k + shift, spread[k * size_y : (k + 1) * size_y], total)
        out_ref[place, place_rows] = total


def y_kernel(data_ref, high_ref, low_ref, out_ref):
    high, low = high_ref[...], low_ref[...]
    lane = lane_of((512, LANES))
    sign = jnp.where(lane // 16 % 2 == 0, 1.0, -1.0).astype(F32)
    swap = lane ^ 16
    back = lane // 16 * 16 + (16 - lane % 16) % 16

    def transformed(values):
        first, rest = split(values)
        return dot(high, first) + (dot(high, rest) + dot(low, first))

    def turned(products):
        return permuted(products, swap) * sign

    border = data_ref[:, 256:272]
    moved = pltpu.roll(border.reshape(256, LANES), LANES - 8, 1).reshape(16, 16, LANES)
    products = transformed(jnp.concatenate([border, moved], 1).reshape(512, LANES))
    extra = (products[:512] - turned(products[512:])) * sign
    for step in range(4):
        pair = (2 * step, 2 * step + 1)
        values = jnp.concatenate([data_ref[:, 32 * k : 32 * (k + 1)].reshape(512, LANES) for k in pair], 1)
        products = transformed(values)
        for place, k in enumerate(pair):
            cos_part = products[:512, LANES * place : LANES * (place + 1)]
            sin_part = turned(products[512:, LANES * place : LANES * (place + 1)])
            rows = pl.ds(32 * k, 32)
            out_ref[:, 0, rows] = (cos_part + sin_part).reshape(16, 32, LANES)
            mirrored = permuted((cos_part - sin_part) * sign, back)
            edge = extra if k == 0 else pltpu.roll(extra, LANES - k, 1)
            out_ref[:, 1, rows] = jnp.where(lane % 16 == 0, edge, mirrored).reshape(16, 32, LANES)


def signed_freq(counter, length):
    shifted = (counter + length // 2) % length - length // 2
    return shifted.astype(F32) / (length / 2.0)


def x_kernel(data_ref, high_ref, low_ref, solid_hbm, orient_hbm, cross_hbm, solid_ref, orient_ref, cross_ref, first_ref, rest_ref, sems):
    py, pz = lax.axis_index("py"), lax.axis_index("pz")
    flip = (pz >= 8).astype(jnp.int32)
    high, low = high_ref[...], low_ref[...]
    kx = lax.broadcasted_iota(jnp.int32, (32, 256), 1)
    kz = lax.broadcasted_iota(jnp.int32, (32, 256), 0) + pz * 32
    plane = jnp.exp(-0.5 * (signed_freq(kx, 256) ** 2 + signed_freq(kz, 512) ** 2)) * (1.0 / 67108864.0)
    copies = []
    for step in range(32 // STEP_KY):
        for own in range(STEP_KY):
            ky = step * STEP_KY + own
            for half in range(2):
                rows = [data_ref[source, half ^ flip, pl.ds(ky, 8, stride=32), :] for source in range(16)]
                turned = jnp.concatenate(rows, 0).T
                joined = jnp.concatenate([turned[:64], turned[64:]], 1)
                first, rest = split(joined)
                start = own * 128 + half * 64
                first_ref[step % 2, start : start + 64] = first
                rest_ref[step % 2, start : start + 64] = rest
        first, rest = first_ref[step % 2], rest_ref[step % 2]
        products = dot(first, high) + (dot(first, low) + dot(rest, high))
        for own in range(STEP_KY):
            ky = step * STEP_KY + own
            index = jnp.full((1, 256), py * 32 + ky, jnp.int32)
            weight = plane * jnp.exp(-0.5 * signed_freq(index, 512) ** 2)
            weight = jnp.where((kx == 0) & (kz == 0) & (index == 0), 0.0, weight)
            for half in range(2):
                start = own * 128 + half * 64
                cos_part = [products[start + 16 * i : start + 16 * (i + 1), :256] for i in range(4)]
                sin_part = [products[start + 16 * i : start + 16 * (i + 1), 256:] for i in range(4)]
                solid_re = cos_part[0] + sin_part[1]
                solid_im = cos_part[1] - sin_part[0]
                orient_re = cos_part[2] + sin_part[3]
                orient_im = cos_part[3] - sin_part[2]
                scaled = weight[16 * half : 16 * (half + 1)]
                where = pl.ds(16 * half, 16)
                solid_ref[ky, where] = scaled * (solid_re * solid_re + solid_im * solid_im)
                orient_ref[ky, where] = scaled * (orient_re * orient_re + orient_im * orient_im)
                cross_ref[0, ky, where] = scaled * (solid_re * orient_re + solid_im * orient_im)
                cross_ref[1, ky, where] = scaled * (solid_im * orient_re - solid_re * orient_im)
        done = pl.ds(step * STEP_KY, STEP_KY)
        pairs = ((solid_ref.at[done], solid_hbm.at[done]), (orient_ref.at[done], orient_hbm.at[done]), (cross_ref.at[:, done], cross_hbm.at[:, done]))
        for number, (source, target) in enumerate(pairs):
            copy = pltpu.make_async_copy(source, target, sems.at[3 * step + number])
            copy.start()
            copies.append(copy)
    for copy in copies:
        copy.wait()


def whole(shape):
    return pl.BlockSpec(shape, lambda *_: (0,) * len(shape))


IN_VMEM = pl.BlockSpec(memory_space=pltpu.VMEM)
IN_HBM = pl.BlockSpec(memory_space=pltpu.HBM)


def body(solid, orientation):
    params = pltpu.CompilerParams(vmem_limit_bytes=VMEM_LIMIT)
    z_params = pltpu.CompilerParams(vmem_limit_bytes=52 * 1024 * 1024)
    z_high, z_low = z_tables()
    by_y = pl.BlockSpec((16, STEP_Y, 512), lambda i: (0, i, 0))
    field = pl.pallas_call(
        z_kernel,
        grid=(32 // STEP_Y,),
        in_specs=[by_y, by_y, whole(z_high.shape), whole(z_low.shape)],
        out_specs=IN_VMEM,
        out_shape=pltpu.VMEM((16, 272, LANES), F32),
        compiler_params=z_params,
        name="z_transform",
    )(solid, orientation, z_high, z_low)
    field = lax.all_to_all(field, "pz", 0, 0, tiled=True)
    y_high, y_low = y_tables()
    field = pl.pallas_call(
        y_kernel,
        in_specs=[IN_VMEM] * 3,
        out_specs=IN_VMEM,
        out_shape=pltpu.VMEM((16, 2, 256, LANES), F32),
        compiler_params=params,
        name="y_transform",
    )(field, y_high, y_low)
    groups = [[py * 16 + pz for py in range(16) for pz in (low, 15 - low)] for low in range(8)]
    field = lax.all_to_all(
        field.reshape(32, 256, LANES), ("py", "pz"), 0, 0, tiled=True, axis_index_groups=groups
    ).reshape(16, 2, 256, LANES)
    x_high, x_low = x_tables()
    out = jax.ShapeDtypeStruct((32, 32, 256), F32)
    wide = jax.ShapeDtypeStruct((2, 32, 32, 256), F32)
    steps = 32 // STEP_KY
    return tuple(
        pl.pallas_call(
            x_kernel,
            in_specs=[IN_VMEM] * 3,
            out_specs=[IN_HBM] * 3,
            out_shape=[out, out, wide],
            scratch_shapes=[
                pltpu.VMEM(out.shape, F32),
                pltpu.VMEM(out.shape, F32),
                pltpu.VMEM(wide.shape, F32),
                pltpu.VMEM((2, STEP_KY * 128, 256), BF16),
                pltpu.VMEM((2, STEP_KY * 128, 256), BF16),
                pltpu.SemaphoreType.DMA((3 * steps,)),
            ],
            compiler_params=params,
            name="x_transform",
        )(field, x_high, x_low)
    )


def solution(mesh):
    placed = (P("py", "pz", None), P("py", "pz", None))
    return jax.shard_map(
        body,
        mesh=mesh,
        in_specs=placed,
        out_specs=(P("py", "pz", None), P("py", "pz", None), P(None, "py", "pz", None)),
        check_vma=False,
    )
```

```python
import jax
import jax.numpy as jnp
import numpy as np
from jax import lax
from jax.experimental import pallas as pl
from jax.experimental.pallas import tpu as pltpu
from jax.sharding import PartitionSpec as P

F32 = jnp.float32
BF16 = jnp.bfloat16
LANES = 128
VMEM_LIMIT = 36 * 1024 * 1024
STEP_Y = 16
STEP_KY = 2


def two_parts(table):
    high = np.asarray(table, np.float32).astype(jnp.bfloat16)
    low = (np.asarray(table, np.float64) - high.astype(np.float64)).astype(np.float32).astype(jnp.bfloat16)
    return high, low


def cos_sin(rows, columns, length):
    angles = (np.outer(rows, columns) % length) * (2.0 * np.pi / length)
    return np.cos(angles), np.sin(angles)


def first_kz(place):
    return 32 * place if place < 8 else 32 * (15 - place) + 16


def z_tables():
    z = np.arange(512)
    regular, extra = [], []
    for place in range(16):
        cos, sin = cos_sin(z, first_kz(place) + np.arange(17), 512)
        regular += [cos[:, :16], -sin[:, :16]]
        extra.append((cos[:, 16:], -sin[:, 16:]))
    spread = [pair[part] for part in range(2) for pair in extra]
    return two_parts(np.concatenate(regular + spread * 4, 1))


def y_tables():
    tables = []
    for parity in range(2):
        cos, sin = cos_sin(np.arange(256), 2 * np.arange(256) + parity, 512)
        tables.append(np.concatenate([cos, sin], 0))
    return two_parts(np.stack(tables))


def x_tables():
    half, source, low = np.meshgrid(np.arange(2), np.arange(16), np.arange(8), indexing="ij")
    x = (source * 16 + half * 8 + low).reshape(-1)
    cos, sin = cos_sin(x, np.arange(256), 256)
    return two_parts(np.concatenate([cos, sin], 1))


def split(values):
    high = values.astype(BF16)
    return high, (values - high.astype(F32)).astype(BF16)


def dot(a, b):
    return jnp.dot(a, b, preferred_element_type=F32)


def lane_of(shape):
    return lax.broadcasted_iota(jnp.int32, shape, len(shape) - 1)


def permuted(values, source_lane):
    return jnp.take_along_axis(values, source_lane, axis=1, mode="promise_in_bounds")


def z_kernel(solid_ref, orient_ref, high_ref, low_ref, out_ref):
    size_y = STEP_Y
    rows = 8 * size_y
    chunks = 32 // size_y
    i = pl.program_id(0)
    high, low = high_ref[...], low_ref[...]
    lane = lane_of((rows, LANES))
    group = lane // 32

    def gathered(items):
        return jnp.where(group == 0, items[0], jnp.where(group == 1, items[1], jnp.where(group == 2, items[2], items[3])))

    spot = lane_of((size_y, LANES)) % 16
    solid = solid_ref[...].reshape(2 * rows, 512).astype(F32).astype(BF16)
    orient, rest = split(orient_ref[...].reshape(2 * rows, 512))
    both = jnp.concatenate([solid, orient], 0)
    small = dot(both, low)
    large = dot(jnp.concatenate([both, rest], 0), high)
    solid_z = large[: 2 * rows] + small[: 2 * rows]
    orient_z = large[2 * rows : 4 * rows] + (small[2 * rows :] + large[4 * rows :])
    pieces = (solid_z[:rows], orient_z[:rows], solid_z[rows:], orient_z[rows:])
    first = pl.multiple_of(i * size_y, 8)
    for tile in range(4):
        columns = [piece[:, LANES * tile : LANES * (tile + 1)] for piece in pieces]
        for q in range(4):
            moved = [columns[c] if c == q else pltpu.roll(columns[c], 32 * (c - q) % LANES, 1) for c in range(4)]
            ready = gathered(moved)
            for k in range(8):
                out_ref[4 * tile + q, pl.ds(32 * k + first, size_y)] = ready[k * size_y : (k + 1) * size_y]
    extra = gathered([piece[:, 512:640] for piece in pieces])
    shift = 8 * (2 * i // chunks)
    place_rows = pl.ds(pl.multiple_of(256 + i * size_y % 16, 8), size_y)
    sixteen = lane_of((size_y, LANES)) // 16 * 16
    turned = [permuted(extra[k * size_y : (k + 1) * size_y], sixteen + (spot - k) % 16) for k in range(8)]
    ours = (spot >= shift) & (spot < shift + 8)
    for place in range(16):
        mixed = turned[0]
        for k in range(1, 8):
            mixed = jnp.where(spot == (place + k) % 16, turned[k], mixed)
        mixed = permuted(mixed, sixteen + (spot + (place - shift)) % 16)
        before = jnp.where(shift == 0, 0.0, out_ref[place, place_rows])
        out_ref[place, place_rows] = jnp.where(ours, mixed, before)


def y_kernel(data_ref, high_ref, low_ref, out_ref):
    lane = lane_of((256, LANES))
    sign = jnp.where(lane // 16 % 2 == 0, 1.0, -1.0).astype(F32)
    swap = lane ^ 16
    back = lane // 16 * 16 + (16 - lane % 16) % 16

    def transformed(values, parity):
        first, rest = split(values)
        high, low = high_ref[parity], low_ref[parity]
        return dot(high, first) + (dot(high, rest) + dot(low, first))

    def turned(products):
        return permuted(products, swap) * sign

    def halves(even, odd):
        cos_even, cos_odd, sin_even, sin_odd = even[:256], odd[:256], even[256:], odd[256:]
        return (cos_even + cos_odd, sin_even + sin_odd), (cos_even - cos_odd, sin_even - sin_odd)

    def border(parity):
        rows = data_ref[:, pl.ds(256 + parity, 8, stride=2), :]
        moved = pltpu.roll(rows.reshape(LANES, LANES), LANES - 8, 1).reshape(16, 8, LANES)
        return transformed(jnp.concatenate([rows, moved], 1).reshape(256, LANES), parity)

    def pair_of(step, parity):
        parts = [data_ref[:, pl.ds(32 * k + parity, 16, stride=2), :].reshape(256, LANES) for k in (2 * step, 2 * step + 1)]
        return transformed(jnp.concatenate(parts, 1), parity)

    extra = [(cos_part - turned(sin_part)) * sign for cos_part, sin_part in halves(border(0), border(1))]
    for step in range(4):
        both = halves(pair_of(step, 0), pair_of(step, 1))
        for half in range(2):
            for place in range(2):
                k = 2 * step + place
                cos_part, sin_part = [part[:, LANES * place : LANES * (place + 1)] for part in both[half]]
                sin_part = turned(sin_part)
                targets, rows = pl.ds(8 * half, 8), pl.ds(32 * k, 32)
                out_ref[targets, 0, rows] = (cos_part + sin_part).reshape(8, 32, LANES)
                mirrored = permuted((cos_part - sin_part) * sign, back)
                edge = extra[half] if k == 0 else pltpu.roll(extra[half], LANES - k, 1)
                out_ref[targets, 1, rows] = jnp.where(lane % 16 == 0, edge, mirrored).reshape(8, 32, LANES)


def signed_freq(counter, length):
    shifted = (counter + length // 2) % length - length // 2
    return shifted.astype(F32) / (length / 2.0)


def x_kernel(data_ref, high_ref, low_ref, solid_hbm, orient_hbm, cross_hbm, solid_ref, orient_ref, cross_ref, first_ref, rest_ref, sems):
    py, pz = lax.axis_index("py"), lax.axis_index("pz")
    flip = (pz >= 8).astype(jnp.int32)
    high, low = high_ref[...], low_ref[...]
    kx = lax.broadcasted_iota(jnp.int32, (32, 256), 1)
    kz = lax.broadcasted_iota(jnp.int32, (32, 256), 0) + pz * 32
    plane = jnp.exp(-0.5 * (signed_freq(kx, 256) ** 2 + signed_freq(kz, 512) ** 2)) * (1.0 / 67108864.0)
    copies = []
    for step in range(32 // STEP_KY):
        for own in range(STEP_KY):
            ky = step * STEP_KY + own
            for half in range(2):
                rows = [data_ref[source, half ^ flip, pl.ds(ky, 8, stride=32), :] for source in range(16)]
                turned = jnp.concatenate(rows, 0).T
                joined = jnp.concatenate([turned[:64], turned[64:]], 1)
                first, rest = split(joined)
                start = own * 128 + half * 64
                first_ref[step % 2, start : start + 64] = first
                rest_ref[step % 2, start : start + 64] = rest
        first, rest = first_ref[step % 2], rest_ref[step % 2]
        products = dot(first, high) + (dot(first, low) + dot(rest, high))
        for own in range(STEP_KY):
            ky = step * STEP_KY + own
            index = jnp.full((1, 256), py * 32 + ky, jnp.int32)
            weight = plane * jnp.exp(-0.5 * signed_freq(index, 512) ** 2)
            weight = jnp.where((kx == 0) & (kz == 0) & (index == 0), 0.0, weight)
            for half in range(2):
                start = own * 128 + half * 64
                cos_part = [products[start + 16 * i : start + 16 * (i + 1), :256] for i in range(4)]
                sin_part = [products[start + 16 * i : start + 16 * (i + 1), 256:] for i in range(4)]
                solid_re = cos_part[0] + sin_part[1]
                solid_im = cos_part[1] - sin_part[0]
                orient_re = cos_part[2] + sin_part[3]
                orient_im = cos_part[3] - sin_part[2]
                scaled = weight[16 * half : 16 * (half + 1)]
                where = pl.ds(16 * half, 16)
                solid_ref[ky, where] = scaled * (solid_re * solid_re + solid_im * solid_im)
                orient_ref[ky, where] = scaled * (orient_re * orient_re + orient_im * orient_im)
                cross_ref[0, ky, where] = scaled * (solid_re * orient_re + solid_im * orient_im)
                cross_ref[1, ky, where] = scaled * (solid_im * orient_re - solid_re * orient_im)
        done = pl.ds(step * STEP_KY, STEP_KY)
        pairs = ((solid_ref.at[done], solid_hbm.at[done]), (orient_ref.at[done], orient_hbm.at[done]), (cross_ref.at[:, done], cross_hbm.at[:, done]))
        for number, (source, target) in enumerate(pairs):
            copy = pltpu.make_async_copy(source, target, sems.at[3 * step + number])
            copy.start()
            copies.append(copy)
    for copy in copies:
        copy.wait()


def whole(shape):
    return pl.BlockSpec(shape, lambda *_: (0,) * len(shape))


IN_VMEM = pl.BlockSpec(memory_space=pltpu.VMEM)
IN_HBM = pl.BlockSpec(memory_space=pltpu.HBM)


def body(solid, orientation):
    params = pltpu.CompilerParams(vmem_limit_bytes=VMEM_LIMIT)
    z_params = pltpu.CompilerParams(vmem_limit_bytes=52 * 1024 * 1024)
    z_high, z_low = z_tables()
    by_y = pl.BlockSpec((16, STEP_Y, 512), lambda i: (0, i, 0))
    field = pl.pallas_call(
        z_kernel,
        grid=(32 // STEP_Y,),
        in_specs=[by_y, by_y, whole(z_high.shape), whole(z_low.shape)],
        out_specs=IN_VMEM,
        out_shape=pltpu.VMEM((16, 272, LANES), F32),
        compiler_params=z_params,
        name="z_transform",
    )(solid, orientation, z_high, z_low)
    field = lax.all_to_all(field, "pz", 0, 0, tiled=True)
    y_high, y_low = y_tables()
    field = pl.pallas_call(
        y_kernel,
        in_specs=[IN_VMEM] * 3,
        out_specs=IN_VMEM,
        out_shape=pltpu.VMEM((16, 2, 256, LANES), F32),
        compiler_params=params,
        name="y_transform",
    )(field, y_high, y_low)
    groups = [[py * 16 + pz for py in range(16) for pz in (low, 15 - low)] for low in range(8)]
    field = lax.all_to_all(
        field.reshape(32, 256, LANES), ("py", "pz"), 0, 0, tiled=True, axis_index_groups=groups
    ).reshape(16, 2, 256, LANES)
    x_high, x_low = x_tables()
    out = jax.ShapeDtypeStruct((32, 32, 256), F32)
    wide = jax.ShapeDtypeStruct((2, 32, 32, 256), F32)
    steps = 32 // STEP_KY
    return tuple(
        pl.pallas_call(
            x_kernel,
            in_specs=[IN_VMEM] * 3,
            out_specs=[IN_HBM] * 3,
            out_shape=[out, out, wide],
            scratch_shapes=[
                pltpu.VMEM(out.shape, F32),
                pltpu.VMEM(out.shape, F32),
                pltpu.VMEM(wide.shape, F32),
                pltpu.VMEM((2, STEP_KY * 128, 256), BF16),
                pltpu.VMEM((2, STEP_KY * 128, 256), BF16),
                pltpu.SemaphoreType.DMA((3 * steps,)),
            ],
            compiler_params=params,
            name="x_transform",
        )(field, x_high, x_low)
    )


def solution(mesh):
    placed = (P("py", "pz", None), P("py", "pz", None))
    return jax.shard_map(
        body,
        mesh=mesh,
        in_specs=placed,
        out_specs=(P("py", "pz", None), P("py", "pz", None), P(None, "py", "pz", None)),
        check_vma=False,
    )
```

```python
import jax
import jax.numpy as jnp
import numpy as np
from jax import lax
from jax.experimental import pallas as pl
from jax.experimental.pallas import tpu as pltpu
from jax.sharding import PartitionSpec as P

F32 = jnp.float32
BF16 = jnp.bfloat16
LANES = 128
VMEM_LIMIT = 36 * 1024 * 1024
STEP_Y = 16
STEP_KY = 4


def two_parts(table):
    high = np.asarray(table, np.float32).astype(jnp.bfloat16)
    low = (np.asarray(table, np.float64) - high.astype(np.float64)).astype(np.float32).astype(jnp.bfloat16)
    return high, low


def cos_sin(rows, columns, length):
    angles = (np.outer(rows, columns) % length) * (2.0 * np.pi / length)
    return np.cos(angles), np.sin(angles)


def first_kz(place):
    return 32 * place if place < 8 else 32 * (15 - place) + 16


def z_tables():
    z = np.arange(512)
    regular, extra = [], []
    for place in range(16):
        cos, sin = cos_sin(z, first_kz(place) + np.arange(17), 512)
        regular += [cos[:, :16], -sin[:, :16]]
        extra.append((cos[:, 16:], -sin[:, 16:]))
    spread = [pair[part] for part in range(2) for pair in extra]
    return two_parts(np.concatenate(regular + spread * 4, 1))


def y_tables():
    tables = []
    for parity in range(2):
        cos, sin = cos_sin(np.arange(256), 2 * np.arange(256) + parity, 512)
        tables.append(np.concatenate([cos, sin], 0))
    return two_parts(np.stack(tables))


def x_tables():
    half, source, low = np.meshgrid(np.arange(2), np.arange(16), np.arange(8), indexing="ij")
    x = (source * 16 + half * 8 + low).reshape(-1)
    cos, sin = cos_sin(x, np.arange(129), 256)
    return two_parts(np.concatenate([cos[:, :128], cos[:, 128:], sin[:, 1:128]], 1))


def split(values):
    high = values.astype(BF16)
    return high, (values - high.astype(F32)).astype(BF16)


def dot(a, b):
    return jnp.dot(a, b, preferred_element_type=F32)


def lane_of(shape):
    return lax.broadcasted_iota(jnp.int32, shape, len(shape) - 1)


def permuted(values, source_lane):
    return jnp.take_along_axis(values, source_lane, axis=1, mode="promise_in_bounds")


def z_kernel(solid_ref, orient_ref, high_ref, low_ref, out_ref):
    size_y = STEP_Y
    rows = 8 * size_y
    chunks = 32 // size_y
    i = pl.program_id(0)
    high, low = high_ref[...], low_ref[...]
    lane = lane_of((rows, LANES))
    group = lane // 32

    def gathered(items):
        return jnp.where(group == 0, items[0], jnp.where(group == 1, items[1], jnp.where(group == 2, items[2], items[3])))

    spot = lane_of((size_y, LANES)) % 16
    solid = solid_ref[...].reshape(2 * rows, 512).astype(F32).astype(BF16)
    orient, rest = split(orient_ref[...].reshape(2 * rows, 512))
    both = jnp.concatenate([solid, orient], 0)
    small = dot(both, low)
    large = dot(jnp.concatenate([both, rest], 0), high)
    solid_z = large[: 2 * rows] + small[: 2 * rows]
    orient_z = large[2 * rows : 4 * rows] + (small[2 * rows :] + large[4 * rows :])
    pieces = (solid_z[:rows], orient_z[:rows], solid_z[rows:], orient_z[rows:])
    first = pl.multiple_of(i * size_y, 8)
    for tile in range(4):
        columns = [piece[:, LANES * tile : LANES * (tile + 1)] for piece in pieces]
        for q in range(4):
            moved = [columns[c] if c == q else pltpu.roll(columns[c], 32 * (c - q) % LANES, 1) for c in range(4)]
            ready = gathered(moved)
            for k in range(8):
                out_ref[4 * tile + q, pl.ds(32 * k + first, size_y)] = ready[k * size_y : (k + 1) * size_y]
    extra = gathered([piece[:, 512:640] for piece in pieces])
    shift = 8 * (2 * i // chunks)
    place_rows = pl.ds(pl.multiple_of(256 + i * size_y % 16, 8), size_y)
    sixteen = lane_of((size_y, LANES)) // 16 * 16
    turned = [permuted(extra[k * size_y : (k + 1) * size_y], sixteen + (spot - k) % 16) for k in range(8)]
    ours = (spot >= shift) & (spot < shift + 8)
    for place in range(16):
        mixed = turned[0]
        for k in range(1, 8):
            mixed = jnp.where(spot == (place + k) % 16, turned[k], mixed)
        mixed = permuted(mixed, sixteen + (spot + (place - shift)) % 16)
        before = jnp.where(shift == 0, 0.0, out_ref[place, place_rows])
        out_ref[place, place_rows] = jnp.where(ours, mixed, before)


def y_kernel(data_ref, high_ref, low_ref, out_ref):
    lane = lane_of((256, LANES))
    sign = jnp.where(lane // 16 % 2 == 0, 1.0, -1.0).astype(F32)
    swap = lane ^ 16
    back = lane // 16 * 16 + (16 - lane % 16) % 16

    def transformed(values, parity):
        first, rest = split(values)
        high, low = high_ref[parity], low_ref[parity]
        return dot(high, first) + (dot(high, rest) + dot(low, first))

    def turned(products):
        return permuted(products, swap) * sign

    def halves(even, odd):
        cos_even, cos_odd, sin_even, sin_odd = even[:256], odd[:256], even[256:], odd[256:]
        return (cos_even + cos_odd, sin_even + sin_odd), (cos_even - cos_odd, sin_even - sin_odd)

    def border(parity):
        rows = data_ref[:, pl.ds(256 + parity, 8, stride=2), :]
        moved = pltpu.roll(rows.reshape(LANES, LANES), LANES - 8, 1).reshape(16, 8, LANES)
        return transformed(jnp.concatenate([rows, moved], 1).reshape(256, LANES), parity)

    def pair_of(step, parity):
        parts = [data_ref[:, pl.ds(32 * k + parity, 16, stride=2), :].reshape(256, LANES) for k in (2 * step, 2 * step + 1)]
        return transformed(jnp.concatenate(parts, 1), parity)

    extra = [(cos_part - turned(sin_part)) * sign for cos_part, sin_part in halves(border(0), border(1))]
    for step in range(4):
        both = halves(pair_of(step, 0), pair_of(step, 1))
        for half in range(2):
            for place in range(2):
                k = 2 * step + place
                cos_part, sin_part = [part[:, LANES * place : LANES * (place + 1)] for part in both[half]]
                sin_part = turned(sin_part)
                targets = pl.ds(8 * half, 8)
                out_ref[targets, 0, :, k] = (cos_part + sin_part).reshape(8, 4, 8, LANES)
                mirrored = permuted((cos_part - sin_part) * sign, back)
                edge = extra[half] if k == 0 else pltpu.roll(extra[half], LANES - k, 1)
                out_ref[targets, 1, :, k] = jnp.where(lane % 16 == 0, edge, mirrored).reshape(8, 4, 8, LANES)


def signed_freq(counter, length):
    shifted = (counter + length // 2) % length - length // 2
    return shifted.astype(F32) / (length / 2.0)


def x_kernel(data_ref, high_ref, low_ref, solid_hbm, orient_hbm, cross_hbm, solid_ref, orient_ref, cross_ref, first_ref, rest_ref, sems):
    py, pz = lax.axis_index("py"), lax.axis_index("pz")
    flip = (pz >= 8).astype(jnp.int32)
    high, low = high_ref[...], low_ref[...]
    lane = lane_of((16, LANES))
    edge = lane == 0
    back = (LANES - lane) % LANES
    kx = lane_of((32, LANES))
    kz = lax.broadcasted_iota(jnp.int32, (32, LANES), 0) + pz * 32
    freq_z = signed_freq(kz, 512) ** 2
    planes = [
        jnp.exp(-0.5 * (signed_freq(k, 256) ** 2 + freq_z)) * (1.0 / 67108864.0)
        for k in (kx, jnp.where(kx == 0, 128, kx))
    ]
    origin = (kx == 0) & (kz == 0)
    copies = []
    for step in range(32 // STEP_KY):
        for own in range(STEP_KY):
            ky = step * STEP_KY + own
            for half in range(2):
                rows = [data_ref[source, half ^ flip, pl.ds(ky // 8 * 64 + ky % 8, 8, stride=8), :] for source in range(16)]
                turned = jnp.concatenate(rows, 0).T
                joined = jnp.concatenate([turned[:64], turned[64:]], 1)
                first, rest = split(joined)
                start = own * 128 + half * 64
                first_ref[step % 2, start : start + 64] = first
                rest_ref[step % 2, start : start + 64] = rest
        first, rest = first_ref[step % 2], rest_ref[step % 2]
        products = dot(first, high) + (dot(first, low) + dot(rest, high))
        for own in range(STEP_KY):
            ky = step * STEP_KY + own
            index = jnp.full((1, LANES), py * 32 + ky, jnp.int32)
            own_weight = jnp.exp(-0.5 * signed_freq(index, 512) ** 2)
            weights = (jnp.where(origin & (index == 0), 0.0, planes[0] * own_weight), planes[1] * own_weight)
            for half in range(2):
                start = own * 128 + half * 64
                cos_part = [products[start + 16 * i : start + 16 * (i + 1), :LANES] for i in range(4)]
                sin_part = [products[start + 16 * i : start + 16 * (i + 1), LANES:] for i in range(4)]
                sin_only = [jnp.where(edge, 0.0, part) for part in sin_part]
                where = pl.ds(16 * half, 16)
                for side in range(2):
                    fields = []
                    for re, im in ((0, 1), (2, 3)):
                        if side == 0:
                            fields += [cos_part[re] + sin_only[im], cos_part[im] - sin_only[re]]
                        else:
                            fields += [
                                jnp.where(edge, sin_part[re], cos_part[re] - sin_part[im]),
                                jnp.where(edge, sin_part[im], cos_part[im] + sin_part[re]),
                            ]
                    solid_re, solid_im, orient_re, orient_im = fields
                    scaled = weights[side][16 * half : 16 * (half + 1)]
                    results = [
                        scaled * (solid_re * solid_re + solid_im * solid_im),
                        scaled * (orient_re * orient_re + orient_im * orient_im),
                        scaled * (solid_re * orient_re + solid_im * orient_im),
                        scaled * (solid_im * orient_re - solid_re * orient_im),
                    ]
                    if side == 1:
                        results = [permuted(result, back) for result in results]
                    there = pl.ds(LANES * side, LANES)
                    solid_ref[ky, where, there] = results[0]
                    orient_ref[ky, where, there] = results[1]
                    cross_ref[0, ky, where, there] = results[2]
                    cross_ref[1, ky, where, there] = results[3]
        done = pl.ds(step * STEP_KY, STEP_KY)
        pairs = ((solid_ref.at[done], solid_hbm.at[done]), (orient_ref.at[done], orient_hbm.at[done]), (cross_ref.at[:, done], cross_hbm.at[:, done]))
        for number, (source, target) in enumerate(pairs):
            copy = pltpu.make_async_copy(source, target, sems.at[3 * step + number])
            copy.start()
            copies.append(copy)
    for copy in copies:
        copy.wait()


def whole(shape):
    return pl.BlockSpec(shape, lambda *_: (0,) * len(shape))


IN_VMEM = pl.BlockSpec(memory_space=pltpu.VMEM)
IN_HBM = pl.BlockSpec(memory_space=pltpu.HBM)


def body(solid, orientation):
    params = pltpu.CompilerParams(vmem_limit_bytes=VMEM_LIMIT)
    z_params = pltpu.CompilerParams(vmem_limit_bytes=52 * 1024 * 1024)
    z_high, z_low = z_tables()
    by_y = pl.BlockSpec((16, STEP_Y, 512), lambda i: (0, i, 0))
    field = pl.pallas_call(
        z_kernel,
        grid=(32 // STEP_Y,),
        in_specs=[by_y, by_y, whole(z_high.shape), whole(z_low.shape)],
        out_specs=IN_VMEM,
        out_shape=pltpu.VMEM((16, 272, LANES), F32),
        compiler_params=z_params,
        name="z_transform",
    )(solid, orientation, z_high, z_low)
    field = lax.all_to_all(field, "pz", 0, 0, tiled=True)
    y_high, y_low = y_tables()
    field = pl.pallas_call(
        y_kernel,
        in_specs=[IN_VMEM] * 3,
        out_specs=IN_VMEM,
        out_shape=pltpu.VMEM((16, 2, 4, 8, 8, LANES), F32),
        compiler_params=params,
        name="y_transform",
    )(field, y_high, y_low)
    groups = [[py * 16 + pz for py in range(16) for pz in (low, 15 - low)] for low in range(8)]
    field = lax.all_to_all(
        field.reshape(32, 256, LANES), ("py", "pz"), 0, 0, tiled=True, axis_index_groups=groups
    ).reshape(16, 2, 256, LANES)
    x_high, x_low = x_tables()
    out = jax.ShapeDtypeStruct((32, 32, 256), F32)
    wide = jax.ShapeDtypeStruct((2, 32, 32, 256), F32)
    steps = 32 // STEP_KY
    return tuple(
        pl.pallas_call(
            x_kernel,
            in_specs=[IN_VMEM] * 3,
            out_specs=[IN_HBM] * 3,
            out_shape=[out, out, wide],
            scratch_shapes=[
                pltpu.VMEM(out.shape, F32),
                pltpu.VMEM(out.shape, F32),
                pltpu.VMEM(wide.shape, F32),
                pltpu.VMEM((2, STEP_KY * 128, 256), BF16),
                pltpu.VMEM((2, STEP_KY * 128, 256), BF16),
                pltpu.SemaphoreType.DMA((3 * steps,)),
            ],
            compiler_params=params,
            name="x_transform",
        )(field, x_high, x_low)
    )


def solution(mesh):
    placed = (P("py", "pz", None), P("py", "pz", None))
    return jax.shard_map(
        body,
        mesh=mesh,
        in_specs=placed,
        out_specs=(P("py", "pz", None), P("py", "pz", None), P(None, "py", "pz", None)),
        check_vma=False,
    )
```

```python
import jax
import jax.numpy as jnp
import numpy as np
from jax import lax
from jax.experimental import pallas as pl
from jax.experimental.pallas import tpu as pltpu
from jax.sharding import PartitionSpec as P

F32 = jnp.float32
BF16 = jnp.bfloat16
LANES = 128
VMEM_LIMIT = 36 * 1024 * 1024
STEP_Y = 16
STEP_KY = 4


def two_parts(table):
    high = np.asarray(table, np.float32).astype(jnp.bfloat16)
    low = (np.asarray(table, np.float64) - high.astype(np.float64)).astype(np.float32).astype(jnp.bfloat16)
    return high, low


def cos_sin(rows, columns, length):
    angles = (np.outer(rows, columns) % length) * (2.0 * np.pi / length)
    return np.cos(angles), np.sin(angles)


def first_kz(place):
    return 32 * place if place < 8 else 32 * (15 - place) + 16


def z_tables():
    z = np.arange(256)
    none = np.zeros((256, 256))
    parts = [cos_sin(z, first_kz(place) + np.arange(17), 512) for place in range(16)]
    cos = np.concatenate([part[0][:, :16] for part in parts], 1)
    sin = np.concatenate([part[1][:, :16] for part in parts], 1)
    last_cos = np.concatenate([part[0][:, 16:] for part in parts] + [none[:, :16]], 1)
    last_sin = np.concatenate([none[:, :16]] + [-part[1][:, 16:] for part in parts], 1)
    even, odd = np.concatenate([cos] + [last_cos] * 4, 1), np.concatenate([-sin] + [last_sin] * 4, 1)
    return two_parts(np.stack([even, odd]))


def y_tables():
    tables = []
    for parity in range(2):
        cos, sin = cos_sin(np.arange(256), 2 * np.arange(256) + parity, 512)
        tables.append(np.concatenate([cos, sin], 0))
    return two_parts(np.stack(tables))


def x_tables():
    half, source, low = np.meshgrid(np.arange(2), np.arange(16), np.arange(8), indexing="ij")
    x = (source * 16 + half * 8 + low).reshape(-1)
    cos, sin = cos_sin(x, np.arange(129), 256)
    return two_parts(np.concatenate([cos[:, :128], cos[:, 128:], sin[:, 1:128]], 1))


def split(values):
    high = values.astype(BF16)
    return high, (values - high.astype(F32)).astype(BF16)


def dot(a, b):
    return jnp.dot(a, b, preferred_element_type=F32)


def lane_of(shape):
    return lax.broadcasted_iota(jnp.int32, shape, len(shape) - 1)


def permuted(values, source_lane):
    return jnp.take_along_axis(values, source_lane, axis=1, mode="promise_in_bounds")


def z_kernel(solid_ref, orient_ref, high_ref, low_ref, out_ref):
    size_y = STEP_Y
    rows = 8 * size_y
    chunks = 32 // size_y
    i = pl.program_id(0)
    lane = lane_of((rows, LANES))
    group = lane // 32
    row_lane = lane_of((2 * rows, LANES))
    edge = row_lane == 0
    back = (LANES - row_lane) % LANES

    def gathered(items):
        return jnp.where(group == 0, items[0], jnp.where(group == 1, items[1], jnp.where(group == 2, items[2], items[3])))

    def folded(values):
        parts = [values[:, LANES * n : LANES * (n + 1)] for n in range(4)]
        far, near = permuted(parts[3], back), permuted(parts[2], back)
        facing = jnp.concatenate([jnp.where(edge, 0.0, far), jnp.where(edge, far, near)], 1)
        return values[:, :256] + facing, values[:, :256] - facing, near[:, :1]

    *solids, solid_mid = folded(solid_ref[...].reshape(2 * rows, 512).astype(F32))
    *orients, orient_mid = folded(orient_ref[...].reshape(2 * rows, 512))
    solid_z, orient_z = [], []
    for part in range(2):
        orient, rest = split(orients[part])
        both = jnp.concatenate([solids[part].astype(BF16), orient], 0)
        small = dot(both, low_ref[part])
        large = dot(jnp.concatenate([both, rest], 0), high_ref[part])
        solid_z.append(large[: 2 * rows] + small[: 2 * rows])
        orient_z.append(large[2 * rows : 4 * rows] + (small[2 * rows :] + large[4 * rows :]))
    wide = lane_of((2 * rows, 384))
    share = jnp.where(wide < 256, jnp.where(wide % 2 == 0, 1.0, -1.0), jnp.where(wide // 16 % 2 == 0, 1.0, 0.0))
    solid_z[0] += solid_mid * share
    orient_z[0] += orient_mid * share
    spot = lane_of((size_y, LANES)) % 16
    halves = (slice(0, rows), slice(rows, 2 * rows))
    first = pl.multiple_of(i * size_y, 8)
    for tile in range(2):
        columns = slice(LANES * tile, LANES * (tile + 1))
        blocks = [field[part][half, columns] for half in halves for field in (solid_z, orient_z) for part in range(2)]
        for bit in (1, 2, 4):
            unset = lane // 16 // bit % 2 == 0
            for c in range(8):
                if c & bit == 0:
                    one, two = blocks[c], blocks[c | bit]
                    moving = jnp.where(unset, two, one)
                    moved = pltpu.roll(moving, 64, 1) if bit == 4 else permuted(moving, lane ^ 16 * bit)
                    blocks[c] = jnp.where(unset, one, moved)
                    blocks[c | bit] = jnp.where(unset, moved, two)
        for q in range(8):
            for k in range(8):
                out_ref[8 * tile + q, pl.ds(32 * k + first, size_y)] = blocks[q][k * size_y : (k + 1) * size_y]
    extra = gathered([field[0][half, 256:] + field[1][half, 256:] for half in halves for field in (solid_z, orient_z)])
    shift = 8 * (2 * i // chunks)
    place_rows = pl.ds(pl.multiple_of(256 + i * size_y % 16, 8), size_y)
    sixteen = lane_of((size_y, LANES)) // 16 * 16
    turned = [permuted(extra[k * size_y : (k + 1) * size_y], sixteen + (spot - k) % 16) for k in range(8)]
    ours = (spot >= shift) & (spot < shift + 8)
    for place in range(16):
        mixed = turned[0]
        for k in range(1, 8):
            mixed = jnp.where(spot == (place + k) % 16, turned[k], mixed)
        mixed = permuted(mixed, sixteen + (spot + (place - shift)) % 16)
        before = jnp.where(shift == 0, 0.0, out_ref[place, place_rows])
        out_ref[place, place_rows] = jnp.where(ours, mixed, before)


def y_kernel(data_ref, high_ref, low_ref, out_ref):
    lane = lane_of((256, LANES))
    sign = jnp.where(lane // 16 % 2 == 0, 1.0, -1.0).astype(F32)
    swap = lane ^ 16
    back = lane // 16 * 16 + (16 - lane % 16) % 16

    def transformed(values, parity):
        first, rest = split(values)
        high, low = high_ref[parity], low_ref[parity]
        return dot(high, first) + (dot(high, rest) + dot(low, first))

    def turned(products):
        return permuted(products, swap) * sign

    def halves(even, odd):
        cos_even, cos_odd, sin_even, sin_odd = even[:256], odd[:256], even[256:], odd[256:]
        return (cos_even + cos_odd, sin_even + sin_odd), (cos_even - cos_odd, sin_even - sin_odd)

    def border(parity):
        rows = data_ref[:, pl.ds(256 + parity, 8, stride=2), :]
        moved = pltpu.roll(rows.reshape(LANES, LANES), LANES - 8, 1).reshape(16, 8, LANES)
        return transformed(jnp.concatenate([rows, moved], 1).reshape(256, LANES), parity)

    def pair_of(step, parity):
        parts = [data_ref[:, pl.ds(32 * k + parity, 16, stride=2), :].reshape(256, LANES) for k in (2 * step, 2 * step + 1)]
        return transformed(jnp.concatenate(parts, 1), parity)

    extra = [(cos_part - turned(sin_part)) * sign for cos_part, sin_part in halves(border(0), border(1))]
    for step in range(4):
        both = halves(pair_of(step, 0), pair_of(step, 1))
        for half in range(2):
            for place in range(2):
                k = 2 * step + place
                cos_part, sin_part = [part[:, LANES * place : LANES * (place + 1)] for part in both[half]]
                sin_part = turned(sin_part)
                targets = pl.ds(8 * half, 8)
                out_ref[targets, 0, :, k] = (cos_part + sin_part).reshape(8, 4, 8, LANES)
                mirrored = permuted((cos_part - sin_part) * sign, back)
                edge = extra[half] if k == 0 else pltpu.roll(extra[half], LANES - k, 1)
                out_ref[targets, 1, :, k] = jnp.where(lane % 16 == 0, edge, mirrored).reshape(8, 4, 8, LANES)


def signed_freq(counter, length):
    shifted = (counter + length // 2) % length - length // 2
    return shifted.astype(F32) / (length / 2.0)


def x_kernel(data_ref, high_ref, low_ref, solid_hbm, orient_hbm, cross_hbm, solid_ref, orient_ref, cross_ref, first_ref, rest_ref, sems):
    py, pz = lax.axis_index("py"), lax.axis_index("pz")
    flip = (pz >= 8).astype(jnp.int32)
    high, low = high_ref[...], low_ref[...]
    lane = lane_of((16, LANES))
    edge = lane == 0
    back = (LANES - lane) % LANES
    kx = lane_of((32, LANES))
    kz = lax.broadcasted_iota(jnp.int32, (32, LANES), 0) + pz * 32
    freq_z = signed_freq(kz, 512) ** 2
    planes = [
        jnp.exp(-0.5 * (signed_freq(k, 256) ** 2 + freq_z)) * (1.0 / 67108864.0)
        for k in (kx, jnp.where(kx == 0, 128, kx))
    ]
    origin = (kx == 0) & (kz == 0)
    copies = []
    for step in range(32 // STEP_KY):
        for own in range(STEP_KY):
            ky = step * STEP_KY + own
            for half in range(2):
                rows = [data_ref[source, half ^ flip, pl.ds(ky // 8 * 64 + ky % 8, 8, stride=8), :] for source in range(16)]
                turned = jnp.concatenate(rows, 0).T
                joined = jnp.concatenate([turned[:64], turned[64:]], 1)
                first, rest = split(joined)
                start = own * 128 + half * 64
                first_ref[step % 2, start : start + 64] = first
                rest_ref[step % 2, start : start + 64] = rest
        first, rest = first_ref[step % 2], rest_ref[step % 2]
        products = dot(first, high) + (dot(first, low) + dot(rest, high))
        for own in range(STEP_KY):
            ky = step * STEP_KY + own
            index = jnp.full((1, LANES), py * 32 + ky, jnp.int32)
            own_weight = jnp.exp(-0.5 * signed_freq(index, 512) ** 2)
            weights = (jnp.where(origin & (index == 0), 0.0, planes[0] * own_weight), planes[1] * own_weight)
            for half in range(2):
                start = own * 128 + half * 64
                cos_part = [products[start + 16 * i : start + 16 * (i + 1), :LANES] for i in range(4)]
                sin_part = [products[start + 16 * i : start + 16 * (i + 1), LANES:] for i in range(4)]
                sin_only = [jnp.where(edge, 0.0, part) for part in sin_part]
                where = pl.ds(16 * half, 16)
                for side in range(2):
                    fields = []
                    for re, im in ((0, 1), (2, 3)):
                        if side == 0:
                            fields += [cos_part[re] + sin_only[im], cos_part[im] - sin_only[re]]
                        else:
                            fields += [
                                jnp.where(edge, sin_part[re], cos_part[re] - sin_part[im]),
                                jnp.where(edge, sin_part[im], cos_part[im] + sin_part[re]),
                            ]
                    solid_re, solid_im, orient_re, orient_im = fields
                    scaled = weights[side][16 * half : 16 * (half + 1)]
                    results = [
                        scaled * (solid_re * solid_re + solid_im * solid_im),
                        scaled * (orient_re * orient_re + orient_im * orient_im),
                        scaled * (solid_re * orient_re + solid_im * orient_im),
                        scaled * (solid_im * orient_re - solid_re * orient_im),
                    ]
                    if side == 1:
                        results = [permuted(result, back) for result in results]
                    there = pl.ds(LANES * side, LANES)
                    solid_ref[ky, where, there] = results[0]
                    orient_ref[ky, where, there] = results[1]
                    cross_ref[0, ky, where, there] = results[2]
                    cross_ref[1, ky, where, there] = results[3]
        done = pl.ds(step * STEP_KY, STEP_KY)
        pairs = ((solid_ref.at[done], solid_hbm.at[done]), (orient_ref.at[done], orient_hbm.at[done]), (cross_ref.at[:, done], cross_hbm.at[:, done]))
        for number, (source, target) in enumerate(pairs):
            copy = pltpu.make_async_copy(source, target, sems.at[3 * step + number])
            copy.start()
            copies.append(copy)
    for copy in copies:
        copy.wait()


def whole(shape):
    return pl.BlockSpec(shape, lambda *_: (0,) * len(shape))


IN_VMEM = pl.BlockSpec(memory_space=pltpu.VMEM)
IN_HBM = pl.BlockSpec(memory_space=pltpu.HBM)


def body(solid, orientation):
    params = pltpu.CompilerParams(vmem_limit_bytes=VMEM_LIMIT)
    z_params = pltpu.CompilerParams(vmem_limit_bytes=52 * 1024 * 1024)
    z_high, z_low = z_tables()
    by_y = pl.BlockSpec((16, STEP_Y, 512), lambda i: (0, i, 0))
    field = pl.pallas_call(
        z_kernel,
        grid=(32 // STEP_Y,),
        in_specs=[by_y, by_y, whole(z_high.shape), whole(z_low.shape)],
        out_specs=IN_VMEM,
        out_shape=pltpu.VMEM((16, 272, LANES), F32),
        compiler_params=z_params,
        name="z_transform",
    )(solid, orientation, z_high, z_low)
    field = lax.all_to_all(field, "pz", 0, 0, tiled=True)
    y_high, y_low = y_tables()
    field = pl.pallas_call(
        y_kernel,
        in_specs=[IN_VMEM] * 3,
        out_specs=IN_VMEM,
        out_shape=pltpu.VMEM((16, 2, 4, 8, 8, LANES), F32),
        compiler_params=params,
        name="y_transform",
    )(field, y_high, y_low)
    groups = [[py * 16 + pz for py in range(16) for pz in (low, 15 - low)] for low in range(8)]
    field = lax.all_to_all(
        field.reshape(32, 256, LANES), ("py", "pz"), 0, 0, tiled=True, axis_index_groups=groups
    ).reshape(16, 2, 256, LANES)
    x_high, x_low = x_tables()
    out = jax.ShapeDtypeStruct((32, 32, 256), F32)
    wide = jax.ShapeDtypeStruct((2, 32, 32, 256), F32)
    steps = 32 // STEP_KY
    return tuple(
        pl.pallas_call(
            x_kernel,
            in_specs=[IN_VMEM] * 3,
            out_specs=[IN_HBM] * 3,
            out_shape=[out, out, wide],
            scratch_shapes=[
                pltpu.VMEM(out.shape, F32),
                pltpu.VMEM(out.shape, F32),
                pltpu.VMEM(wide.shape, F32),
                pltpu.VMEM((2, STEP_KY * 128, 256), BF16),
                pltpu.VMEM((2, STEP_KY * 128, 256), BF16),
                pltpu.SemaphoreType.DMA((3 * steps,)),
            ],
            compiler_params=params,
            name="x_transform",
        )(field, x_high, x_low)
    )


def solution(mesh):
    placed = (P("py", "pz", None), P("py", "pz", None))
    return jax.shard_map(
        body,
        mesh=mesh,
        in_specs=placed,
        out_specs=(P("py", "pz", None), P("py", "pz", None), P(None, "py", "pz", None)),
        check_vma=False,
    )
```

```python
import jax
import jax.numpy as jnp
import numpy as np
from jax import lax
from jax.experimental import pallas as pl
from jax.experimental.pallas import tpu as pltpu
from jax.sharding import PartitionSpec as P

F32 = jnp.float32
BF16 = jnp.bfloat16
LANES = 128
VMEM_LIMIT = 36 * 1024 * 1024
STEP_Y = 16
STEP_KY = 4


def two_parts(table):
    high = np.asarray(table, np.float32).astype(jnp.bfloat16)
    low = (np.asarray(table, np.float64) - high.astype(np.float64)).astype(np.float32).astype(jnp.bfloat16)
    return high, low


def cos_sin(rows, columns, length):
    angles = (np.outer(rows, columns) % length) * (2.0 * np.pi / length)
    return np.cos(angles), np.sin(angles)


def first_kz(place):
    return 32 * place if place < 8 else 32 * (15 - place) + 16


def z_tables():
    z = np.arange(256)
    none = np.zeros((256, 256))
    parts = [cos_sin(z, first_kz(place) + np.arange(17), 512) for place in range(16)]
    cos = np.concatenate([part[0][:, :16] for part in parts], 1)
    sin = np.concatenate([part[1][:, :16] for part in parts], 1)
    last_cos = np.concatenate([part[0][:, 16:] for part in parts] + [none[:, :16]], 1)
    last_sin = np.concatenate([none[:, :16]] + [-part[1][:, 16:] for part in parts], 1)
    even, odd = np.concatenate([cos] + [last_cos] * 4, 1), np.concatenate([-sin] + [last_sin] * 4, 1)
    return two_parts(np.stack([even, odd]))


def y_tables():
    tables = []
    for parity in range(2):
        cos, sin = cos_sin(np.arange(256), 2 * np.arange(256) + parity, 512)
        tables.append(np.concatenate([cos, sin], 0))
    return two_parts(np.stack(tables))


def x_tables():
    half, source, low = np.meshgrid(np.arange(2), np.arange(16), np.arange(8), indexing="ij")
    x = (source * 16 + half * 8 + low).reshape(-1)
    cos, sin = cos_sin(x, np.arange(129), 256)
    return two_parts(np.concatenate([cos[:, :128], cos[:, 128:], sin[:, 1:128]], 1))


def split(values):
    high = values.astype(BF16)
    return high, (values - high.astype(F32)).astype(BF16)


def dot(a, b):
    return jnp.dot(a, b, preferred_element_type=F32)


def lane_of(shape):
    return lax.broadcasted_iota(jnp.int32, shape, len(shape) - 1)


def permuted(values, source_lane):
    return jnp.take_along_axis(values, source_lane, axis=1, mode="promise_in_bounds")


def z_kernel(solid_ref, orient_ref, high_ref, low_ref, out_ref):
    size_y = STEP_Y
    rows = 8 * size_y
    chunks = 32 // size_y
    i = pl.program_id(0)
    lane = lane_of((rows, LANES))
    group = lane // 32
    row_lane = lane_of((2 * rows, LANES))
    edge = row_lane == 0
    back = (LANES - row_lane) % LANES

    def gathered(items):
        return jnp.where(group == 0, items[0], jnp.where(group == 1, items[1], jnp.where(group == 2, items[2], items[3])))

    def folded(values):
        parts = [values[:, LANES * n : LANES * (n + 1)] for n in range(4)]
        far, near = permuted(parts[3], back), permuted(parts[2], back)
        facing = jnp.concatenate([jnp.where(edge, 0.0, far), jnp.where(edge, far, near)], 1)
        return values[:, :256] + facing, values[:, :256] - facing, near[:, :1]

    *solids, solid_mid = folded(solid_ref[...].reshape(2 * rows, 512).astype(F32))
    *orients, orient_mid = folded(orient_ref[...].reshape(2 * rows, 512))
    solid_z, orient_z = [], []
    for part in range(2):
        orient, rest = split(orients[part])
        both = jnp.concatenate([solids[part].astype(BF16), orient], 0)
        small = dot(both, low_ref[part])
        large = dot(jnp.concatenate([both, rest], 0), high_ref[part])
        solid_z.append(large[: 2 * rows] + small[: 2 * rows])
        orient_z.append(large[2 * rows : 4 * rows] + (small[2 * rows :] + large[4 * rows :]))
    wide = lane_of((2 * rows, 384))
    share = jnp.where(wide < 256, jnp.where(wide % 2 == 0, 1.0, -1.0), jnp.where(wide // 16 % 2 == 0, 1.0, 0.0))
    solid_z[0] += solid_mid * share
    orient_z[0] += orient_mid * share
    spot = lane_of((size_y, LANES)) % 16
    halves = (slice(0, rows), slice(rows, 2 * rows))
    first = pl.multiple_of(i * size_y, 8)
    for tile in range(2):
        columns = slice(LANES * tile, LANES * (tile + 1))
        blocks = [field[part][half, columns] for half in halves for field in (solid_z, orient_z) for part in range(2)]
        for bit in (1, 2, 4):
            unset = lane // 16 // bit % 2 == 0
            for c in range(8):
                if c & bit == 0:
                    one, two = blocks[c], blocks[c | bit]
                    moving = jnp.where(unset, two, one)
                    moved = pltpu.roll(moving, 64, 1) if bit == 4 else permuted(moving, lane ^ 16 * bit)
                    blocks[c] = jnp.where(unset, one, moved)
                    blocks[c | bit] = jnp.where(unset, moved, two)
        for q in range(8):
            for k in range(8):
                out_ref[8 * tile + q, pl.ds(32 * k + first, size_y)] = blocks[q][k * size_y : (k + 1) * size_y]
    extra = gathered([field[0][half, 256:] + field[1][half, 256:] for half in halves for field in (solid_z, orient_z)])
    shift = 8 * (2 * i // chunks)
    place_rows = pl.ds(pl.multiple_of(256 + i * size_y % 16, 8), size_y)
    sixteen = lane_of((size_y, LANES)) // 16 * 16
    turned = [permuted(extra[k * size_y : (k + 1) * size_y], sixteen + (spot - k) % 16) for k in range(8)]
    ours = (spot >= shift) & (spot < shift + 8)
    for place in range(16):
        mixed = turned[0]
        for k in range(1, 8):
            mixed = jnp.where(spot == (place + k) % 16, turned[k], mixed)
        mixed = permuted(mixed, sixteen + (spot + (place - shift)) % 16)
        before = jnp.where(shift == 0, 0.0, out_ref[place, place_rows])
        out_ref[place, place_rows] = jnp.where(ours, mixed, before)


def y_kernel(data_ref, high_ref, low_ref, out_ref):
    lane = lane_of((256, LANES))
    sign = jnp.where(lane // 16 % 2 == 0, 1.0, -1.0).astype(F32)
    swap = lane ^ 16
    back = lane // 16 * 16 + (16 - lane % 16) % 16

    def transformed(values, parity):
        first, rest = split(values)
        high, low = high_ref[parity], low_ref[parity]
        return dot(high, first) + (dot(high, rest) + dot(low, first))

    def turned(products):
        return permuted(products, swap) * sign

    def halves(even, odd):
        cos_even, cos_odd, sin_even, sin_odd = even[:256], odd[:256], even[256:], odd[256:]
        return (cos_even + cos_odd, sin_even + sin_odd), (cos_even - cos_odd, sin_even - sin_odd)

    def border(parity):
        rows = data_ref[:, pl.ds(256 + parity, 8, stride=2), :]
        moved = pltpu.roll(rows.reshape(LANES, LANES), LANES - 8, 1).reshape(16, 8, LANES)
        return transformed(jnp.concatenate([rows, moved], 1).reshape(256, LANES), parity)

    def pair_of(step, parity):
        parts = [data_ref[:, pl.ds(32 * k + parity, 16, stride=2), :].reshape(256, LANES) for k in (2 * step, 2 * step + 1)]
        return transformed(jnp.concatenate(parts, 1), parity)

    extra = [(cos_part - turned(sin_part)) * sign for cos_part, sin_part in halves(border(0), border(1))]
    for step in range(4):
        both = halves(pair_of(step, 0), pair_of(step, 1))
        for half in range(2):
            for place in range(2):
                k = 2 * step + place
                cos_part, sin_part = [part[:, LANES * place : LANES * (place + 1)] for part in both[half]]
                sin_part = turned(sin_part)
                targets = pl.ds(8 * half, 8)
                out_ref[0, targets, :, k] = (cos_part + sin_part).reshape(8, 4, 8, LANES)
                mirrored = permuted((cos_part - sin_part) * sign, back)
                edge = extra[half] if k == 0 else pltpu.roll(extra[half], LANES - k, 1)
                out_ref[1, targets, :, k] = jnp.where(lane % 16 == 0, edge, mirrored).reshape(8, 4, 8, LANES)


def signed_freq(counter, length):
    shifted = (counter + length // 2) % length - length // 2
    return shifted.astype(F32) / (length / 2.0)


def x_kernel(data_ref, high_ref, low_ref, solid_hbm, orient_hbm, cross_hbm, solid_ref, orient_ref, cross_ref, first_ref, rest_ref, sems):
    py, pz = lax.axis_index("py"), lax.axis_index("pz")
    flip = (pz >= 8).astype(jnp.int32)
    high, low = high_ref[...], low_ref[...]
    lane = lane_of((16, LANES))
    edge = lane == 0
    back = (LANES - lane) % LANES
    kx = lane_of((32, LANES))
    kz = lax.broadcasted_iota(jnp.int32, (32, LANES), 0) + pz * 32
    freq_z = signed_freq(kz, 512) ** 2
    planes = [
        jnp.exp(-0.5 * (signed_freq(k, 256) ** 2 + freq_z)) * (1.0 / 67108864.0)
        for k in (kx, jnp.where(kx == 0, 128, kx))
    ]
    origin = (kx == 0) & (kz == 0)
    copies = []
    for step in range(32 // STEP_KY):
        for own in range(STEP_KY):
            ky = step * STEP_KY + own
            for half in range(2):
                rows = [data_ref[half ^ flip, source, pl.ds(ky // 8 * 64 + ky % 8, 8, stride=8), :] for source in range(16)]
                turned = jnp.concatenate(rows, 0).T
                joined = jnp.concatenate([turned[:64], turned[64:]], 1)
                first, rest = split(joined)
                start = own * 128 + half * 64
                first_ref[step % 2, start : start + 64] = first
                rest_ref[step % 2, start : start + 64] = rest
        first, rest = first_ref[step % 2], rest_ref[step % 2]
        products = dot(first, high) + (dot(first, low) + dot(rest, high))
        for own in range(STEP_KY):
            ky = step * STEP_KY + own
            index = jnp.full((1, LANES), py * 32 + ky, jnp.int32)
            own_weight = jnp.exp(-0.5 * signed_freq(index, 512) ** 2)
            weights = (jnp.where(origin & (index == 0), 0.0, planes[0] * own_weight), planes[1] * own_weight)
            for half in range(2):
                start = own * 128 + half * 64
                cos_part = [products[start + 16 * i : start + 16 * (i + 1), :LANES] for i in range(4)]
                sin_part = [products[start + 16 * i : start + 16 * (i + 1), LANES:] for i in range(4)]
                sin_only = [jnp.where(edge, 0.0, part) for part in sin_part]
                where = pl.ds(16 * half, 16)
                for side in range(2):
                    fields = []
                    for re, im in ((0, 1), (2, 3)):
                        if side == 0:
                            fields += [cos_part[re] + sin_only[im], cos_part[im] - sin_only[re]]
                        else:
                            fields += [
                                jnp.where(edge, sin_part[re], cos_part[re] - sin_part[im]),
                                jnp.where(edge, sin_part[im], cos_part[im] + sin_part[re]),
                            ]
                    solid_re, solid_im, orient_re, orient_im = fields
                    scaled = weights[side][16 * half : 16 * (half + 1)]
                    results = [
                        scaled * (solid_re * solid_re + solid_im * solid_im),
                        scaled * (orient_re * orient_re + orient_im * orient_im),
                        scaled * (solid_re * orient_re + solid_im * orient_im),
                        scaled * (solid_im * orient_re - solid_re * orient_im),
                    ]
                    if side == 1:
                        results = [permuted(result, back) for result in results]
                    there = pl.ds(LANES * side, LANES)
                    solid_ref[ky, where, there] = results[0]
                    orient_ref[ky, where, there] = results[1]
                    cross_ref[0, ky, where, there] = results[2]
                    cross_ref[1, ky, where, there] = results[3]
        done = pl.ds(step * STEP_KY, STEP_KY)
        pairs = ((solid_ref.at[done], solid_hbm.at[done]), (orient_ref.at[done], orient_hbm.at[done]), (cross_ref.at[:, done], cross_hbm.at[:, done]))
        for number, (source, target) in enumerate(pairs):
            copy = pltpu.make_async_copy(source, target, sems.at[3 * step + number])
            copy.start()
            copies.append(copy)
    for copy in copies:
        copy.wait()


def whole(shape):
    return pl.BlockSpec(shape, lambda *_: (0,) * len(shape))


IN_VMEM = pl.BlockSpec(memory_space=pltpu.VMEM)
IN_HBM = pl.BlockSpec(memory_space=pltpu.HBM)


def body(solid, orientation):
    params = pltpu.CompilerParams(vmem_limit_bytes=VMEM_LIMIT)
    z_params = pltpu.CompilerParams(vmem_limit_bytes=52 * 1024 * 1024)
    z_high, z_low = z_tables()
    by_y = pl.BlockSpec((16, STEP_Y, 512), lambda i: (0, i, 0))
    field = pl.pallas_call(
        z_kernel,
        grid=(32 // STEP_Y,),
        in_specs=[by_y, by_y, whole(z_high.shape), whole(z_low.shape)],
        out_specs=IN_VMEM,
        out_shape=pltpu.VMEM((16, 272, LANES), F32),
        compiler_params=z_params,
        name="z_transform",
    )(solid, orientation, z_high, z_low)
    field = lax.all_to_all(field, "pz", 0, 0, tiled=True)
    y_high, y_low = y_tables()
    field = pl.pallas_call(
        y_kernel,
        in_specs=[IN_VMEM] * 3,
        out_specs=IN_VMEM,
        out_shape=pltpu.VMEM((2, 16, 4, 8, 8, LANES), F32),
        compiler_params=params,
        name="y_transform",
    )(field, y_high, y_low)
    groups = [[py * 16 + pz for pz in (low, 15 - low) for py in range(16)] for low in range(8)]
    field = lax.all_to_all(
        field.reshape(32, 256, LANES), ("py", "pz"), 0, 0, tiled=True, axis_index_groups=groups
    ).reshape(2, 16, 256, LANES)
    x_high, x_low = x_tables()
    out = jax.ShapeDtypeStruct((32, 32, 256), F32)
    wide = jax.ShapeDtypeStruct((2, 32, 32, 256), F32)
    steps = 32 // STEP_KY
    return tuple(
        pl.pallas_call(
            x_kernel,
            in_specs=[IN_VMEM] * 3,
            out_specs=[IN_HBM] * 3,
            out_shape=[out, out, wide],
            scratch_shapes=[
                pltpu.VMEM(out.shape, F32),
                pltpu.VMEM(out.shape, F32),
                pltpu.VMEM(wide.shape, F32),
                pltpu.VMEM((2, STEP_KY * 128, 256), BF16),
                pltpu.VMEM((2, STEP_KY * 128, 256), BF16),
                pltpu.SemaphoreType.DMA((3 * steps,)),
            ],
            compiler_params=params,
            name="x_transform",
        )(field, x_high, x_low)
    )


def solution(mesh):
    placed = (P("py", "pz", None), P("py", "pz", None))
    return jax.shard_map(
        body,
        mesh=mesh,
        in_specs=placed,
        out_specs=(P("py", "pz", None), P("py", "pz", None), P(None, "py", "pz", None)),
        check_vma=False,
    )
```
